1024 devices in a mesh: replica: 16 (over y, core), fsdp: 64 (over x, z).
Axes of the slice: x: 8, y: 8, z: 8, core: 2. Of those that a mesh axis runs over, the one named last changes fastest.
Arguments:
- grad_part: bfloat16 [16, 64, 7168, 128], P('replica', None, 'fsdp'), may hold values from -6 to 6
- momentum: float32 [64, 7168, 128], P('replica', 'fsdp'), may hold values from -24 to 24
- row_counts: int32 [64], replicated, may hold values from 512 to 7168, as said below
Outputs:
- new_momentum: float32 [64, 7168, 128], P('replica', 'fsdp')
- update: bfloat16 [64, 7168, 128], P('replica', 'fsdp')
The draws below stay inside these ranges and needn't reach their ends.
Inputs may be any that keep to these rules, and one draw needn't show every extreme that they name: `row_counts`: each matrix has 7168 rows (an output projection head) or 512 rows (a key or value head); both kinds occur.
All inputs are finite; a program needn't handle non-finite values.
Results may differ from the reference program's by a relative error of at most 0.04.
Values may be sent and summed in bfloat16 or wider, within the bound.
A program may use at most 32 MiB of HBM per device.

```python
import jax
import jax.numpy as jnp
from jax import lax

D = 7168
HD = 128
KVR = 512
ITERS = 3
MATS = 64
N_REPLICA = 16


def draw_row_counts(key, part):
    key = jax.random.fold_in(key, 1)
    order = jax.random.permutation(key, MATS)
    return jnp.where(order % 3 == 0, D, KVR).astype(jnp.int32)


def with_spikes(array, own_key, source, target, parts, factor):
    owner, partner = [(jnp.arange(array.shape[dim]) // (array.shape[dim] // parts)).reshape([-1 if axis == dim else 1 for axis in range(array.ndim)]) for dim in (source, target)]
    chosen = jax.random.permutation(own_key, parts)[partner]
    strong = (owner == chosen) | (owner == (partner + parts // 2) % parts)
    return jnp.where(strong, factor * array, array)


def shard_levels(key, extent, shards, smallest, high):
    def one(position, parts):
        heights = jax.random.uniform(jax.random.fold_in(jax.random.fold_in(key, 6), position), (parts,), jnp.float32, smallest / len(shards), high / len(shards))
        return jnp.repeat(jnp.exp(heights), extent[position] // parts).reshape((-1,) + (1,) * (len(extent) - position - 1))

    factor_of = one(*shards[0])
    for cut in shards[1:]:
        factor_of = factor_of * one(*cut)
    return factor_of


def centred(stream_key, dims, spread, most, split=(), held_as=jnp.bfloat16):
    result = spread * jax.random.normal(stream_key, dims, jnp.float32)
    if split:
        result = result * shard_levels(stream_key, dims, split, -0.22, 0.18)
    return jnp.clip(result, -most, most).astype(held_as)


def bell_draw_with(rng, shape, scale, reach, cuts, heavy, kind=jnp.bfloat16):
    drawn = scale * jax.random.normal(rng, shape, jnp.float32)
    if cuts:
        drawn = drawn * shard_levels(rng, shape, cuts, -0.22, 0.18)
    return jnp.clip(with_spikes(drawn, jax.random.fold_in(rng, 3), *heavy), -reach, reach).astype(kind)


def setup_inputs(seed: int = 0) -> dict:
    key_of = jax.random.split(jax.random.key(seed), 4)
    return {
        "grad_part": bell_draw_with(key_of[0], (N_REPLICA, MATS, D, HD), 1.0, 6.0, ((0, 16), (2, 64)), (0, 1, 16, 2.0)),
        "momentum": centred(key_of[1], (MATS, D, HD), 4.0, 24.0, ((0, 16), (1, 64)), jnp.float32),
        "row_counts": draw_row_counts(jax.random.fold_in(key_of[3], 71), 0),
    }


def newton(xmat):
    for step in range(ITERS):
        gram = jnp.dot(xmat.T, xmat, preferred_element_type=jnp.float32).astype(jnp.bfloat16)
        poly = (-4.775 * gram.astype(jnp.float32) + 2.0315 * jnp.dot(gram, gram, preferred_element_type=jnp.float32)).astype(jnp.bfloat16)
        xmat = (3.4445 * xmat.astype(jnp.float32) + jnp.dot(xmat, poly, preferred_element_type=jnp.float32)).astype(jnp.bfloat16)
    return xmat

def reference(grad_part, momentum, row_counts):
    grad = lax.optimization_barrier(jnp.sum(grad_part.astype(jnp.float32), axis=0))
    rows = jnp.arange(D, dtype=jnp.int32)
    live = rows[None, :, None] < row_counts[:, None, None]
    new_momentum = jnp.where(live, 0.95 * momentum + grad, jnp.float32(0.0))
    rounded = new_momentum.astype(jnp.bfloat16)
    wide = rounded.astype(jnp.float32)
    norms = jnp.sqrt(lax.optimization_barrier(jnp.sum(wide * wide, axis=(1, 2))))
    start = (wide / (norms[:, None, None] + 1e-07)).astype(jnp.bfloat16)
    ortho = lax.map(newton, start)
    scale = 0.2 * jnp.sqrt(row_counts.astype(jnp.float32))
    update = (ortho.astype(jnp.float32) * scale[:, None, None]).astype(jnp.bfloat16)
    return (new_momentum, update)
```

```python
import functools

import jax
import jax.numpy as jnp
from jax import lax
from jax.experimental import pallas as pl
from jax.experimental.pallas import tpu as pltpu
from jax.sharding import PartitionSpec as P

ITERS = 3
MESH = pl.DeviceIdType.MESH
F32 = jnp.float32
BF16 = jnp.bfloat16
COEF = (3.4445, -4.775, 2.0315)


def ring_messages(ring, mats):
    slots = {}
    for matrix in range(mats):
        for hops in range(ring // 2, 0, -1):
            for way in (0, 1):
                if hops < ring // 2 or matrix % 2 == way:
                    slots[way, hops, matrix] = len(slots)
    return slots


def split(a):
    high = a.astype(BF16)
    return high, (a - high.astype(F32)).astype(BF16)


def product(a, b):
    a_high, a_low = split(a)
    b_high, b_low = split(b)
    return jnp.dot(
        jnp.concatenate([a_high, a_low, a_high], axis=1),
        jnp.concatenate([b_high, b_high, b_low], axis=0),
        preferred_element_type=F32,
    )


def polynomials(grams, eye):
    total = None
    for step in range(ITERS):
        squares = [product(g, g) for g in grams]
        factors = [COEF[0] * eye + COEF[1] * g + COEF[2] * s for g, s in zip(grams, squares)]
        if step < ITERS - 1:
            halves = [product(g, f) for g, f in zip(grams, factors)]
            grams = [product(h, f) for h, f in zip(halves, factors)]
        total = factors if total is None else [product(t, f) for t, f in zip(total, factors)]
    return total


def kernel(
    ring,
    side,
    slots,
    grad,
    momentum,
    row_counts,
    new_momentum,
    update,
    own,
    sib,
    stage,
    landed,
    mom,
    new_mom,
    rounded,
    result,
    counts,
    packed,
    parts1,
    chunk1,
    parts2,
    chunk2,
    full,
    load_sem,
    out_sem,
    sib_send,
    sib_recv,
    ring_send,
    ring_recv,
    sum_send,
    sum_recv,
):
    mats, rows, cols = mom.shape
    half = cols // 2
    part = chunk1.shape[1]
    replica = lax.axis_index("replica")
    fsdp = lax.axis_index("fsdp")
    y, core = replica // 2, lax.rem(replica, 2)
    x, z = fsdp // side, lax.rem(fsdp, side)
    sibling = (2 * y + 1 - core, fsdp)
    ahead = (2 * lax.rem(y + 1, ring) + core, fsdp)
    behind = (2 * lax.rem(y + ring - 1, ring) + core, fsdp)

    def along(axis, d):
        if axis == 0:
            return (replica, lax.rem(x + d, side) * side + z)
        return (replica, x * side + lax.rem(z + d, side))

    barrier = pltpu.get_barrier_semaphore()
    peers = [sibling, ahead, behind]
    peers += [along(axis, d) for axis in (0, 1) for d in range(1, side)]
    for peer in peers:
        pl.semaphore_signal(barrier, inc=1, device_id=peer, device_id_type=MESH)

    order = [ring // 2]
    for hops in range(ring // 2 - 1, 0, -1):
        order += [hops, ring - hops]
    order += [0]

    def chunk_of(o, which):
        return pl.ds((2 * lax.rem(y + o, ring) + which) * mats, mats)

    loads = {}
    for o in order:
        loads[o] = pltpu.make_async_copy(
            grad.at[0, chunk_of(o, core)], own.at[o], load_sem.at[o]
        )
        loads[o].start()
    load_mom = pltpu.make_async_copy(momentum, mom, load_sem.at[ring])
    load_mom.start()
    load_counts = pltpu.make_async_copy(row_counts, counts, load_sem.at[ring + 1])
    load_counts.start()

    pl.semaphore_wait(barrier, len(peers))

    exchange = {}
    for o in order:
        exchange[o] = pltpu.make_async_remote_copy(
            src_ref=grad.at[0, chunk_of(o, 1 - core)],
            dst_ref=sib.at[o],
            send_sem=sib_send.at[o],
            recv_sem=sib_recv.at[o],
            device_id=sibling,
            device_id_type=MESH,
        )
        exchange[o].start()

    ready = set()

    def pair_sum(o, j):
        if o not in ready:
            loads[o].wait()
            exchange[o].wait_recv()
            ready.add(o)
        return own[o, j].astype(F32) + sib[o, j].astype(F32)

    hop = {}

    def ring_step(hops, chosen):
        for j in chosen:
            for way in (0, 1):
                slot = slots.get((way, hops, j))
                if slot is None:
                    continue
                value = pair_sum(hops if way == 0 else ring - hops, j)
                before = slots.get((way, hops + 1, j))
                if before is not None:
                    hop[before].wait_recv()
                    value = value + landed[before].astype(F32)
                stage[slot] = value.astype(BF16)
                hop[slot] = pltpu.make_async_remote_copy(
                    src_ref=stage.at[slot],
                    dst_ref=landed.at[slot],
                    send_sem=ring_send.at[slot],
                    recv_sem=ring_recv.at[slot],
                    device_id=(ahead, behind)[way],
                    device_id_type=MESH,
                )
                hop[slot].start()

    outs = []
    row = fsdp * rows + lax.broadcasted_iota(jnp.int32, (rows, cols), 0)
    lane = lax.broadcasted_iota(jnp.int32, (half, cols), 1)
    left = lane < half
    eye = (
        lax.broadcasted_iota(jnp.int32, (cols, cols), 0)
        == lax.broadcasted_iota(jnp.int32, (cols, cols), 1)
    ).astype(F32)

    def finish_sum(j):
        value = pair_sum(0, j)
        for way in (0, 1):
            slot = slots[way, 1, j]
            hop[slot].wait_recv()
            value = value + landed[slot].astype(F32)
        moved = jnp.where(row < counts[replica * mats + j], 0.95 * mom[j] + value, 0.0)
        new_mom[j] = moved
        out = pltpu.make_async_copy(new_mom.at[j], new_momentum.at[j], out_sem.at[j])
        out.start()
        outs.append(out)
        r = moved.astype(BF16)
        rounded[j] = r
        return lax.dot_general(r, r, (((0,), (0,)), ((), ())), preferred_element_type=F32)

    sends = []

    def send_sum(a, phase, d, src, dst, axis):
        at = (a * 3 + phase) * (side - 1) + d - 1
        copy = pltpu.make_async_remote_copy(
            src_ref=src,
            dst_ref=dst,
            send_sem=sum_send.at[at],
            recv_sem=sum_recv.at[at],
            device_id=along(axis, d),
            device_id_type=MESH,
        )
        copy.start()
        sends.append(copy)
        return copy

    def piece(index):
        return pl.ds(pl.multiple_of(index * part, 8), part)

    flight = {}

    def place(axis):
        return x if axis == 0 else z

    def sum_scatter(a, first, second):
        packed[a, :half] = jnp.where(left, first[:half], first[half:])
        packed[a, half : 2 * half] = jnp.where(left, second[:half], second[half:])
        packed[a, 2 * half :] = jnp.where(left, first[half:], second[:half])
        flight[a] = [
            send_sum(
                a,
                0,
                d,
                packed.at[a, piece(lax.rem(place(a) + d, side))],
                parts1.at[a, d - 1],
                a,
            )
            for d in range(1, side)
        ]

    def sum_across(a):
        value = packed[a, piece(place(a))]
        for d in range(1, side):
            flight[a][d - 1].wait_recv()
            value = value + parts1[a, d - 1]
        chunk1[a] = value
        flight[a] = [
            send_sum(a, 1, d, chunk1.at[a], parts2.at[a, d - 1], 1 - a) for d in range(1, side)
        ]

    def sum_gather(a):
        value = chunk1[a]
        for d in range(1, side):
            flight[a][d - 1].wait_recv()
            value = value + parts2[a, d - 1]
        chunk2[a] = value
        flight[a] = [
            send_sum(a, 2, d, chunk2.at[a], full.at[a, piece(place(a))], a)
            for d in range(1, side)
        ]
        full[a, piece(place(a))] = value

    def finish(a):
        for copy in flight[a]:
            copy.wait_recv()
        first = 0.5 * full[a, :half]
        second = 0.5 * full[a, half : 2 * half]
        cross = full[a, 2 * half :]
        none = jnp.zeros_like(first)
        lower = jnp.concatenate(
            [jnp.where(left, first, none), jnp.where(left, cross, first)], axis=0
        )
        upper = jnp.concatenate(
            [jnp.where(left, second, cross), jnp.where(left, none, second)], axis=0
        )
        grams, scales = [], []
        for i, triangle in enumerate((lower, upper)):
            gram = triangle + triangle.T
            trace = jnp.sum(gram * eye, axis=(0, 1), keepdims=True)
            inverse = 1.0 / (jnp.sqrt(trace) + 1e-07)
            grams.append(gram * inverse * inverse)
            count = jnp.full((1, 1), counts[replica * mats + 2 * a + i], jnp.int32)
            scales.append(0.2 * jnp.sqrt(count.astype(F32)) * inverse)
        for i, whole in enumerate(polynomials(grams, eye)):
            j = 2 * a + i
            high, low = split(whole)
            r = rounded[j]
            value = jnp.dot(
                jnp.concatenate([r, r], axis=1),
                jnp.concatenate([high, low], axis=0),
                preferred_element_type=F32,
            )
            result[j] = (value * scales[i]).astype(BF16)
            out = pltpu.make_async_copy(result.at[j], update.at[j], out_sem.at[mats + j])
            out.start()
            outs.append(out)

    early, late = (0, 1), (2, 3)
    far = ring // 2
    ring_step(far, early)
    ring_step(far - 1, early)
    ring_step(far, late)
    ring_step(far - 2, early)
    ring_step(far - 1, late)
    ring_step(far - 3, early)
    ring_step(far - 2, late)
    load_mom.wait()
    load_counts.wait()
    sum_scatter(0, *[finish_sum(j) for j in early])
    ring_step(far - 3, late)
    sum_across(0)
    sum_scatter(1, *[finish_sum(j) for j in late])
    sum_gather(0)
    sum_across(1)
    finish(0)
    sum_gather(1)
    finish(1)

    for copy in list(exchange.values()) + list(hop.values()) + sends:
        copy.wait_send()
    for out in outs:
        out.wait()


def solution(mesh):
    ring = mesh.shape["replica"] // 2
    side = 8

    def per_device(grad_part, momentum, row_counts):
        mats, rows, cols = momentum.shape
        slots = ring_messages(ring, mats)
        part = 3 * cols // 2 // side
        pairs = mats // 2
        messages = pairs * 3 * (side - 1)
        block = (mats, rows, cols)
        dma = pltpu.SemaphoreType.DMA
        return pl.pallas_call(
            functools.partial(kernel, ring, side, slots),
            out_shape=(
                jax.ShapeDtypeStruct(block, F32),
                jax.ShapeDtypeStruct(block, BF16),
            ),
            in_specs=[pl.BlockSpec(memory_space=pl.ANY)] * 3,
            out_specs=[pl.BlockSpec(memory_space=pl.ANY)] * 2,
            scratch_shapes=[
                pltpu.VMEM((ring,) + block, BF16),
                pltpu.VMEM((ring,) + block, BF16),
                pltpu.VMEM((len(slots), rows, cols), BF16),
                pltpu.VMEM((len(slots), rows, cols), BF16),
                pltpu.VMEM(block, F32),
                pltpu.VMEM(block, F32),
                pltpu.VMEM(block, BF16),
                pltpu.VMEM(block, BF16),
                pltpu.SMEM(row_counts.shape, jnp.int32),
                pltpu.VMEM((pairs, 3 * cols // 2, cols), F32),
                pltpu.VMEM((pairs, side - 1, part, cols), F32),
                pltpu.VMEM((pairs, part, cols), F32),
                pltpu.VMEM((pairs, side - 1, part, cols), F32),
                pltpu.VMEM((pairs, part, cols), F32),
                pltpu.VMEM((pairs, 3 * cols // 2, cols), F32),
                dma((ring + 2,)),
                dma((2 * mats,)),
                dma((ring,)),
                dma((ring,)),
                dma((len(slots),)),
                dma((len(slots),)),
                dma((messages,)),
                dma((messages,)),
            ],
            compiler_params=pltpu.CompilerParams(
                collective_id=0, has_side_effects=True, vmem_limit_bytes=32 * 1024 * 1024
            ),
        )(grad_part, momentum, row_counts)

    return jax.shard_map(
        per_device,
        mesh=mesh,
        in_specs=(P("replica", None, "fsdp", None), P("replica", "fsdp", None), P()),
        out_specs=(P("replica", "fsdp", None), P("replica", "fsdp", None)),
        check_vma=False,
    )
```

```python
import functools

import jax
import jax.numpy as jnp
from jax import lax
from jax.experimental import pallas as pl
from jax.experimental.pallas import tpu as pltpu
from jax.sharding import PartitionSpec as P

ITERS = 3
MESH = pl.DeviceIdType.MESH
F32 = jnp.float32
BF16 = jnp.bfloat16
COEF = (3.4445, -4.775, 2.0315)


THREE_STEPS = {4: 2, 3: 2, 2: 1, 1: 0}
TWO_STEPS = {4: 2, 3: 2, 2: 0, 1: 0}
ROUTES = (THREE_STEPS, THREE_STEPS, TWO_STEPS, TWO_STEPS)
ORDER = (
    (4, (0, 1)),
    (3, (0, 1)),
    (4, (2, 3)),
    (3, (2, 3)),
    (2, (0, 1)),
    (1, (2, 3)),
    (2, (2, 3)),
    (1, (0, 1)),
)


def ring_messages(ring, mats):
    slots = {}
    for matrix in range(mats):
        for hops in range(ring // 2, 0, -1):
            for way in (0, 1):
                if hops < ring // 2 or matrix % 2 == way:
                    slots[way, hops, matrix] = len(slots)
    return slots


def split(a):
    high = a.astype(BF16)
    return high, (a - high.astype(F32)).astype(BF16)


def product(a, b):
    a_high, a_low = split(a)
    b_high, b_low = split(b)
    return jnp.dot(
        jnp.concatenate([a_high, a_low, a_high], axis=1),
        jnp.concatenate([b_high, b_high, b_low], axis=0),
        preferred_element_type=F32,
    )


def iterate(rows, grams, eye):
    total = None
    for step in range(ITERS):
        squares = [product(g, g) for g in grams]
        factors = [COEF[0] * eye + COEF[1] * g + COEF[2] * s for g, s in zip(grams, squares)]
        if step == ITERS - 1:
            break
        halves = [product(g, f) for g, f in zip(grams, factors)]
        grams = [product(h, f) for h, f in zip(halves, factors)]
        total = factors if total is None else [product(t, f) for t, f in zip(total, factors)]
    partly = []
    for r, t in zip(rows, total):
        high, low = split(t)
        partly.append(
            jnp.dot(
                jnp.concatenate([r, r], axis=1),
                jnp.concatenate([high, low], axis=0),
                preferred_element_type=F32,
            )
        )
    return [product(p, f) for p, f in zip(partly, factors)]


def kernel(
    ring,
    side,
    slots,
    grad,
    momentum,
    row_counts,
    new_momentum,
    update,
    own,
    sib,
    stage,
    landed,
    mom,
    new_mom,
    rounded,
    result,
    counts,
    packed,
    parts1,
    chunk1,
    parts2,
    chunk2,
    full,
    load_sem,
    out_sem,
    sib_send,
    sib_recv,
    ring_send,
    ring_recv,
    sum_send,
    sum_recv,
):
    mats, rows, cols = mom.shape
    half = cols // 2
    part = chunk1.shape[1]
    replica = lax.axis_index("replica")
    fsdp = lax.axis_index("fsdp")
    y, core = replica // 2, lax.rem(replica, 2)
    x, z = fsdp // side, lax.rem(fsdp, side)
    sibling = (2 * y + 1 - core, fsdp)

    def along(axis, d):
        if axis == 0:
            return (replica, lax.rem(x + d, side) * side + z)
        return (replica, x * side + lax.rem(z + d, side))

    far_first = sorted(range(1, side), key=lambda d: -min(d, side - d))
    barrier = pltpu.get_barrier_semaphore()
    peers = [sibling]
    peers += [(2 * lax.rem(y + d, ring) + core, fsdp) for d in (1, 2, ring - 2, ring - 1)]
    peers += [along(axis, d) for d in far_first for axis in (0, 1)]
    for peer in peers:
        pl.semaphore_signal(barrier, inc=1, device_id=peer, device_id_type=MESH)

    order = [ring // 2]
    for hops in range(ring // 2 - 1, 0, -1):
        order += [hops, ring - hops]
    order += [0]

    def chunk_of(o, which):
        return pl.ds((2 * lax.rem(y + o, ring) + which) * mats, mats)

    loads = {}
    for o in order:
        loads[o] = pltpu.make_async_copy(
            grad.at[0, chunk_of(o, core)], own.at[o], load_sem.at[o]
        )
        loads[o].start()
    load_mom = pltpu.make_async_copy(momentum, mom, load_sem.at[ring])
    load_mom.start()
    load_counts = pltpu.make_async_copy(row_counts, counts, load_sem.at[ring + 1])
    load_counts.start()

    pl.semaphore_wait(barrier, len(peers))

    exchange = {}
    for o in order:
        exchange[o] = pltpu.make_async_remote_copy(
            src_ref=grad.at[0, chunk_of(o, 1 - core)],
            dst_ref=sib.at[o],
            send_sem=sib_send.at[o],
            recv_sem=sib_recv.at[o],
            device_id=sibling,
            device_id_type=MESH,
        )
        exchange[o].start()

    ready = set()

    def pair_sum(o, j):
        if o not in ready:
            loads[o].wait()
            exchange[o].wait_recv()
            ready.add(o)
        return own[o, j].astype(F32) + sib[o, j].astype(F32)

    hop = {}

    def arrivals(way, hops, j, value):
        for before, after in ROUTES[j].items():
            slot = slots.get((way, before, j))
            if after == hops and slot is not None:
                hop[slot].wait_recv()
                value = value + landed[slot].astype(F32)
        return value

    def ring_step(hops, j):
        for way in (0, 1):
            slot = slots.get((way, hops, j))
            if slot is None:
                continue
            value = arrivals(way, hops, j, pair_sum(hops if way == 0 else ring - hops, j))
            stage[slot] = value.astype(BF16)
            step = hops - ROUTES[j][hops]
            to = lax.rem(y + (step if way == 0 else ring - step), ring)
            hop[slot] = pltpu.make_async_remote_copy(
                src_ref=stage.at[slot],
                dst_ref=landed.at[slot],
                send_sem=ring_send.at[slot],
                recv_sem=ring_recv.at[slot],
                device_id=(2 * to + core, fsdp),
                device_id_type=MESH,
            )
            hop[slot].start()

    outs = []
    row = fsdp * rows + lax.broadcasted_iota(jnp.int32, (rows, cols), 0)
    lane = lax.broadcasted_iota(jnp.int32, (half, cols), 1)
    left = lane < half
    eye = (
        lax.broadcasted_iota(jnp.int32, (cols, cols), 0)
        == lax.broadcasted_iota(jnp.int32, (cols, cols), 1)
    ).astype(F32)

    def finish_sum(j):
        value = pair_sum(0, j)
        for way in (0, 1):
            value = arrivals(way, 0, j, value)
        moved = jnp.where(row < counts[replica * mats + j], 0.95 * mom[j] + value, 0.0)
        new_mom[j] = moved
        out = pltpu.make_async_copy(new_mom.at[j], new_momentum.at[j], out_sem.at[j])
        out.start()
        outs.append(out)
        r = moved.astype(BF16)
        rounded[j] = r
        return lax.dot_general(r, r, (((0,), (0,)), ((), ())), preferred_element_type=F32)

    sends = []

    def send_sum(a, phase, d, src, dst, axis):
        at = (a * 3 + phase) * (side - 1) + d - 1
        copy = pltpu.make_async_remote_copy(
            src_ref=src,
            dst_ref=dst,
            send_sem=sum_send.at[at],
            recv_sem=sum_recv.at[at],
            device_id=along(axis, d),
            device_id_type=MESH,
        )
        copy.start()
        sends.append(copy)
        return copy

    def piece(index):
        return pl.ds(pl.multiple_of(index * part, 8), part)

    flight = {}

    def place(axis):
        return x if axis == 0 else z

    def sum_scatter(a, first, second):
        packed[a, :half] = jnp.where(left, first[:half], first[half:])
        packed[a, half : 2 * half] = jnp.where(left, second[:half], second[half:])
        packed[a, 2 * half :] = jnp.where(left, first[half:], second[:half])
        flight[a] = {
            d: send_sum(
                a,
                0,
                d,
                packed.at[a, piece(lax.rem(place(a) + d, side))],
                parts1.at[a, d - 1],
                a,
            )
            for d in far_first
        }

    def sum_across(a):
        value = packed[a, piece(place(a))]
        for d in reversed(far_first):
            flight[a][d].wait_recv()
            value = value + parts1[a, d - 1]
        chunk1[a] = value
        flight[a] = {
            d: send_sum(a, 1, d, chunk1.at[a], parts2.at[a, d - 1], 1 - a) for d in far_first
        }

    def sum_gather(a):
        value = chunk1[a]
        for d in reversed(far_first):
            flight[a][d].wait_recv()
            value = value + parts2[a, d - 1]
        chunk2[a] = value
        flight[a] = {
            d: send_sum(a, 2, d, chunk2.at[a], full.at[a, piece(place(a))], a) for d in far_first
        }
        full[a, piece(place(a))] = value

    def whole_grams(a):
        for copy in flight[a].values():
            copy.wait_recv()
        first = 0.5 * full[a, :half]
        second = 0.5 * full[a, half : 2 * half]
        cross = full[a, 2 * half :]
        none = jnp.zeros_like(first)
        lower = jnp.concatenate(
            [jnp.where(left, first, none), jnp.where(left, cross, first)], axis=0
        )
        upper = jnp.concatenate(
            [jnp.where(left, second, cross), jnp.where(left, none, second)], axis=0
        )
        return [lower + lower.T, upper + upper.T]

    for hops, chosen in ORDER:
        for j in chosen:
            ring_step(hops, j)
    load_mom.wait()
    load_counts.wait()
    pairs = range(mats // 2)
    for a in pairs:
        sum_scatter(a, finish_sum(2 * a), finish_sum(2 * a + 1))
    for a in pairs:
        sum_across(a)
    for a in pairs:
        sum_gather(a)

    grams, scales = [], []
    for j, gram in enumerate(whole_grams(0) + whole_grams(1)):
        trace = jnp.sum(gram * eye, axis=(0, 1), keepdims=True)
        inverse = 1.0 / (jnp.sqrt(trace) + 1e-07)
        grams.append(gram * inverse * inverse)
        count = jnp.full((1, 1), counts[replica * mats + j], jnp.int32)
        scales.append(0.2 * jnp.sqrt(count.astype(F32)) * inverse)
    for j, value in enumerate(iterate([rounded[j] for j in range(mats)], grams, eye)):
        result[j] = (value * scales[j]).astype(BF16)
        out = pltpu.make_async_copy(result.at[j], update.at[j], out_sem.at[mats + j])
        out.start()
        outs.append(out)

    for copy in list(exchange.values()) + list(hop.values()) + sends:
        copy.wait_send()
    for out in outs:
        out.wait()


def solution(mesh):
    ring = mesh.shape["replica"] // 2
    side = 8

    def per_device(grad_part, momentum, row_counts):
        mats, rows, cols = momentum.shape
        slots = ring_messages(ring, mats)
        part = 3 * cols // 2 // side
        pairs = mats // 2
        messages = pairs * 3 * (side - 1)
        block = (mats, rows, cols)
        dma = pltpu.SemaphoreType.DMA
        return pl.pallas_call(
            functools.partial(kernel, ring, side, slots),
            out_shape=(
                jax.ShapeDtypeStruct(block, F32),
                jax.ShapeDtypeStruct(block, BF16),
            ),
            in_specs=[pl.BlockSpec(memory_space=pl.ANY)] * 3,
            out_specs=[pl.BlockSpec(memory_space=pl.ANY)] * 2,
            scratch_shapes=[
                pltpu.VMEM((ring,) + block, BF16),
                pltpu.VMEM((ring,) + block, BF16),
                pltpu.VMEM((len(slots), rows, cols), BF16),
                pltpu.VMEM((len(slots), rows, cols), BF16),
                pltpu.VMEM(block, F32),
                pltpu.VMEM(block, F32),
                pltpu.VMEM(block, BF16),
                pltpu.VMEM(block, BF16),
                pltpu.SMEM(row_counts.shape, jnp.int32),
                pltpu.VMEM((pairs, 3 * cols // 2, cols), F32),
                pltpu.VMEM((pairs, side - 1, part, cols), F32),
                pltpu.VMEM((pairs, part, cols), F32),
                pltpu.VMEM((pairs, side - 1, part, cols), F32),
                pltpu.VMEM((pairs, part, cols), F32),
                pltpu.VMEM((pairs, 3 * cols // 2, cols), F32),
                dma((ring + 2,)),
                dma((2 * mats,)),
                dma((ring,)),
                dma((ring,)),
                dma((len(slots),)),
                dma((len(slots),)),
                dma((messages,)),
                dma((messages,)),
            ],
            compiler_params=pltpu.CompilerParams(
                collective_id=0, has_side_effects=True, vmem_limit_bytes=60 * 1024 * 1024
            ),
        )(grad_part, momentum, row_counts)

    return jax.shard_map(
        per_device,
        mesh=mesh,
        in_specs=(P("replica", None, "fsdp", None), P("replica", "fsdp", None), P()),
        out_specs=(P("replica", "fsdp", None), P("replica", "fsdp", None)),
        check_vma=False,
    )
```

```python
import functools

import jax
import jax.numpy as jnp
from jax import lax
from jax.experimental import pallas as pl
from jax.experimental.pallas import tpu as pltpu
from jax.sharding import PartitionSpec as P

ITERS = 3
MESH = pl.DeviceIdType.MESH
F32 = jnp.float32
BF16 = jnp.bfloat16
COEF = (3.4445, -4.775, 2.0315)


THREE_STEPS = {4: 2, 3: 2, 2: 1, 1: 0}
TWO_STEPS = {4: 2, 3: 2, 2: 0, 1: 0}
ROUTES = (THREE_STEPS, THREE_STEPS, TWO_STEPS, TWO_STEPS)
ORDER = (
    (4, (0, 1)),
    (3, (0, 1)),
    (4, (2, 3)),
    (3, (2, 3)),
    (2, (0, 1)),
    (1, (2, 3)),
    (2, (2, 3)),
    (1, (0, 1)),
)


def ring_messages(ring, mats):
    slots = {}
    for matrix in range(mats):
        for hops in range(ring // 2, 0, -1):
            for way in (0, 1):
                if hops < ring // 2 or matrix % 2 == way:
                    slots[way, hops, matrix] = len(slots)
    return slots


def split(a):
    high = a.astype(BF16)
    return high, (a - high.astype(F32)).astype(BF16)


def product(a, b):
    a_high, a_low = split(a)
    b_high, b_low = split(b)
    return jnp.dot(
        jnp.concatenate([a_high, a_low, a_high], axis=1),
        jnp.concatenate([b_high, b_high, b_low], axis=0),
        preferred_element_type=F32,
    )


def iterate(rows, grams, eye):
    total = None
    for step in range(ITERS):
        squares = [product(g, g) for g in grams]
        factors = [COEF[0] * eye + COEF[1] * g + COEF[2] * s for g, s in zip(grams, squares)]
        if step == ITERS - 1:
            break
        halves = [product(g, f) for g, f in zip(grams, factors)]
        grams = [product(h, f) for h, f in zip(halves, factors)]
        total = factors if total is None else [product(t, f) for t, f in zip(total, factors)]
    partly = []
    for r, t in zip(rows, total):
        high, low = split(t)
        partly.append(
            jnp.dot(
                jnp.concatenate([r, r], axis=1),
                jnp.concatenate([high, low], axis=0),
                preferred_element_type=F32,
            )
        )
    return [product(p, f) for p, f in zip(partly, factors)]


def kernel(
    ring,
    side,
    slots,
    grad,
    momentum,
    row_counts,
    new_momentum,
    update,
    own,
    sib,
    stage,
    landed,
    mom,
    rounded,
    counts,
    packed,
    parts1,
    chunk1,
    parts2,
    chunk2,
    full,
    load_sem,
    sib_send,
    sib_recv,
    ring_send,
    ring_recv,
    sum_send,
    sum_recv,
):
    mats, rows, cols = mom.shape
    half = cols // 2
    part = chunk1.shape[1]
    replica = lax.axis_index("replica")
    fsdp = lax.axis_index("fsdp")
    y, core = replica // 2, lax.rem(replica, 2)
    x, z = fsdp // side, lax.rem(fsdp, side)
    sibling = (2 * y + 1 - core, fsdp)

    def along(axis, d):
        if axis == 0:
            return (replica, lax.rem(x + d, side) * side + z)
        return (replica, x * side + lax.rem(z + d, side))

    far_first = sorted(range(1, side), key=lambda d: -min(d, side - d))
    barrier = pltpu.get_barrier_semaphore()
    peers = [sibling]
    peers += [(2 * lax.rem(y + d, ring) + core, fsdp) for d in (1, 2, ring - 2, ring - 1)]
    peers += [along(axis, d) for d in far_first for axis in (0, 1)]
    for peer in peers:
        pl.semaphore_signal(barrier, inc=1, device_id=peer, device_id_type=MESH)

    order = [ring // 2]
    for hops in range(ring // 2 - 1, 0, -1):
        order += [hops, ring - hops]
    order += [0]

    def chunk_of(o, which):
        return pl.ds((2 * lax.rem(y + o, ring) + which) * mats, mats)

    loads = {}
    for o in order:
        loads[o] = pltpu.make_async_copy(
            grad.at[0, chunk_of(o, core)], own.at[o], load_sem.at[o]
        )
        loads[o].start()
    load_mom = pltpu.make_async_copy(momentum, mom, load_sem.at[ring])
    load_mom.start()
    load_counts = pltpu.make_async_copy(row_counts, counts, load_sem.at[ring + 1])
    load_counts.start()

    pl.semaphore_wait(barrier, len(peers))

    exchange = {}
    for o in order:
        exchange[o] = pltpu.make_async_remote_copy(
            src_ref=grad.at[0, chunk_of(o, 1 - core)],
            dst_ref=sib.at[o],
            send_sem=sib_send.at[o],
            recv_sem=sib_recv.at[o],
            device_id=sibling,
            device_id_type=MESH,
        )
        exchange[o].start()

    ready = set()

    def pair_sum(o, j):
        if o not in ready:
            loads[o].wait()
            exchange[o].wait_recv()
            ready.add(o)
        return own[o, j].astype(F32) + sib[o, j].astype(F32)

    hop = {}

    def arrivals(way, hops, j, value):
        for before, after in ROUTES[j].items():
            slot = slots.get((way, before, j))
            if after == hops and slot is not None:
                hop[slot].wait_recv()
                value = value + landed[slot].astype(F32)
        return value

    def ring_step(hops, j):
        for way in (0, 1):
            slot = slots.get((way, hops, j))
            if slot is None:
                continue
            value = arrivals(way, hops, j, pair_sum(hops if way == 0 else ring - hops, j))
            stage[slot] = value.astype(BF16)
            step = hops - ROUTES[j][hops]
            to = lax.rem(y + (step if way == 0 else ring - step), ring)
            hop[slot] = pltpu.make_async_remote_copy(
                src_ref=stage.at[slot],
                dst_ref=landed.at[slot],
                send_sem=ring_send.at[slot],
                recv_sem=ring_recv.at[slot],
                device_id=(2 * to + core, fsdp),
                device_id_type=MESH,
            )
            hop[slot].start()

    row = fsdp * rows + lax.broadcasted_iota(jnp.int32, (rows, cols), 0)
    lane = lax.broadcasted_iota(jnp.int32, (half, cols), 1)
    left = lane < half
    eye = (
        lax.broadcasted_iota(jnp.int32, (cols, cols), 0)
        == lax.broadcasted_iota(jnp.int32, (cols, cols), 1)
    ).astype(F32)

    def finish_sum(j):
        value = pair_sum(0, j)
        for way in (0, 1):
            value = arrivals(way, 0, j, value)
        moved = jnp.where(row < counts[replica * mats + j], 0.95 * mom[j] + value, 0.0)
        new_momentum[j] = moved
        r = moved.astype(BF16)
        rounded[j] = r
        return lax.dot_general(r, r, (((0,), (0,)), ((), ())), preferred_element_type=F32)

    sends = []

    def sent():
        while len(sends) > mats // 2 * (side - 1):
            sends.pop(0).wait_send()

    def send_sum(a, phase, d, src, dst, axis):
        at = (a * 3 + phase) * (side - 1) + d - 1
        copy = pltpu.make_async_remote_copy(
            src_ref=src,
            dst_ref=dst,
            send_sem=sum_send.at[at],
            recv_sem=sum_recv.at[at],
            device_id=along(axis, d),
            device_id_type=MESH,
        )
        copy.start()
        sends.append(copy)
        return copy

    def piece(index):
        return pl.ds(pl.multiple_of(index * part, 8), part)

    flight = {}

    def place(axis):
        return x if axis == 0 else z

    def sum_scatter(a, first, second):
        packed[a, :half] = jnp.where(left, first[:half], first[half:])
        packed[a, half : 2 * half] = jnp.where(left, second[:half], second[half:])
        packed[a, 2 * half :] = jnp.where(left, first[half:], second[:half])
        flight[a] = {
            d: send_sum(
                a,
                0,
                d,
                packed.at[a, piece(lax.rem(place(a) + d, side))],
                parts1.at[a, d - 1],
                a,
            )
            for d in far_first
        }

    def sum_across(a):
        value = packed[a, piece(place(a))]
        for d in reversed(far_first):
            flight[a][d].wait_recv()
            value = value + parts1[a, d - 1]
        chunk1[a] = value
        flight[a] = {
            d: send_sum(a, 1, d, chunk1.at[a], parts2.at[a, d - 1], 1 - a) for d in far_first
        }

    def sum_gather(a):
        value = chunk1[a]
        for d in reversed(far_first):
            flight[a][d].wait_recv()
            value = value + parts2[a, d - 1]
        chunk2[a] = value
        flight[a] = {
            d: send_sum(a, 2, d, chunk2.at[a], full.at[a, piece(place(a))], a) for d in far_first
        }
        full[a, piece(place(a))] = value

    def whole_grams(a):
        for copy in flight[a].values():
            copy.wait_recv()
        first = 0.5 * full[a, :half]
        second = 0.5 * full[a, half : 2 * half]
        cross = full[a, 2 * half :]
        none = jnp.zeros_like(first)
        lower = jnp.concatenate(
            [jnp.where(left, first, none), jnp.where(left, cross, first)], axis=0
        )
        upper = jnp.concatenate(
            [jnp.where(left, second, cross), jnp.where(left, none, second)], axis=0
        )
        return [lower + lower.T, upper + upper.T]

    for hops, chosen in ORDER:
        for j in chosen:
            ring_step(hops, j)
    load_mom.wait()
    load_counts.wait()
    pairs = range(mats // 2)
    for a in pairs:
        sum_scatter(a, finish_sum(2 * a), finish_sum(2 * a + 1))
    for copy in list(exchange.values()) + list(hop.values()):
        copy.wait_send()
    for a in pairs:
        sum_across(a)
    sent()
    for a in pairs:
        sum_gather(a)
    sent()

    grams, scales = [], []
    for j, gram in enumerate(whole_grams(0) + whole_grams(1)):
        trace = jnp.sum(gram * eye, axis=(0, 1), keepdims=True)
        inverse = 1.0 / (jnp.sqrt(trace) + 1e-07)
        grams.append(gram * inverse * inverse)
        count = jnp.full((1, 1), counts[replica * mats + j], jnp.int32)
        scales.append(0.2 * jnp.sqrt(count.astype(F32)) * inverse)
    for j, value in enumerate(iterate([rounded[j] for j in range(mats)], grams, eye)):
        update[j] = (value * scales[j]).astype(BF16)

    for copy in sends:
        copy.wait_send()


def solution(mesh):
    ring = mesh.shape["replica"] // 2
    side = 8

    def per_device(grad_part, momentum, row_counts):
        mats, rows, cols = momentum.shape
        slots = ring_messages(ring, mats)
        part = 3 * cols // 2 // side
        pairs = mats // 2
        messages = pairs * 3 * (side - 1)
        block = (mats, rows, cols)
        dma = pltpu.SemaphoreType.DMA
        return pl.pallas_call(
            functools.partial(kernel, ring, side, slots),
            out_shape=(
                pltpu.VMEM(block, F32),
                pltpu.VMEM(block, BF16),
            ),
            in_specs=[pl.BlockSpec(memory_space=pltpu.HBM)] * 3,
            out_specs=[pl.BlockSpec(memory_space=pltpu.VMEM)] * 2,
            scratch_shapes=[
                pltpu.VMEM((ring,) + block, BF16),
                pltpu.VMEM((ring,) + block, BF16),
                pltpu.VMEM((len(slots), rows, cols), BF16),
                pltpu.VMEM((len(slots), rows, cols), BF16),
                pltpu.VMEM(block, F32),
                pltpu.VMEM(block, BF16),
                pltpu.SMEM(row_counts.shape, jnp.int32),
                pltpu.VMEM((pairs, 3 * cols // 2, cols), F32),
                pltpu.VMEM((pairs, side - 1, part, cols), F32),
                pltpu.VMEM((pairs, part, cols), F32),
                pltpu.VMEM((pairs, side - 1, part, cols), F32),
                pltpu.VMEM((pairs, part, cols), F32),
                pltpu.VMEM((pairs, 3 * cols // 2, cols), F32),
                dma((ring + 2,)),
                dma((ring,)),
                dma((ring,)),
                dma((len(slots),)),
                dma((len(slots),)),
                dma((messages,)),
                dma((messages,)),
            ],
            compiler_params=pltpu.CompilerParams(
                collective_id=0, has_side_effects=True, vmem_limit_bytes=60 * 1024 * 1024
            ),
        )(grad_part, momentum, row_counts)

    return jax.shard_map(
        per_device,
        mesh=mesh,
        in_specs=(P("replica", None, "fsdp", None), P("replica", "fsdp", None), P()),
        out_specs=(P("replica", "fsdp", None), P("replica", "fsdp", None)),
        check_vma=False,
    )
```

```python
import functools

import jax
import jax.numpy as jnp
from jax import lax
from jax.experimental import pallas as pl
from jax.experimental.pallas import tpu as pltpu
from jax.sharding import PartitionSpec as P

ITERS = 3
MESH = pl.DeviceIdType.MESH
F32 = jnp.float32
BF16 = jnp.bfloat16
COEF = (3.4445, -4.775, 2.0315)


THREE_STEPS = {4: 2, 3: 2, 2: 1, 1: 0}
TWO_STEPS = {4: 2, 3: 2, 2: 0, 1: 0}
ROUTES = (THREE_STEPS, THREE_STEPS, TWO_STEPS, TWO_STEPS)
ORDER = (
    (4, (0, 1)),
    (3, (0, 1)),
    (4, (2, 3)),
    (3, (2, 3)),
    (2, (0, 1)),
    (1, (2, 3)),
    (2, (2, 3)),
    (1, (0, 1)),
)


def ring_messages(ring, mats):
    slots = {}
    for matrix in range(mats):
        for hops in range(ring // 2, 0, -1):
            for way in (0, 1):
                if hops < ring // 2 or matrix % 2 == way:
                    slots[way, hops, matrix] = len(slots)
    return slots


def split(a):
    high = a.astype(BF16)
    return high, (a - high.astype(F32)).astype(BF16)


def product(a, b):
    a_high, a_low = split(a)
    b_high, b_low = split(b)
    return jnp.dot(
        jnp.concatenate([a_high, a_low, a_high], axis=1),
        jnp.concatenate([b_high, b_high, b_low], axis=0),
        preferred_element_type=F32,
    )


def iterate(rows, grams, eye):
    total = None
    for step in range(ITERS):
        squares = [product(g, g) for g in grams]
        factors = [COEF[0] * eye + COEF[1] * g + COEF[2] * s for g, s in zip(grams, squares)]
        if step == ITERS - 1:
            break
        halves = [product(g, f) for g, f in zip(grams, factors)]
        grams = [product(h, f) for h, f in zip(halves, factors)]
        total = factors if total is None else [product(t, f) for t, f in zip(total, factors)]
    partly = []
    for r, t in zip(rows, total):
        high, low = split(t)
        partly.append(
            jnp.dot(
                jnp.concatenate([r, r], axis=1),
                jnp.concatenate([high, low], axis=0),
                preferred_element_type=F32,
            )
        )
    return [product(p, f) for p, f in zip(partly, factors)]


def kernel(
    ring,
    side,
    slots,
    grad,
    momentum,
    row_counts,
    new_momentum,
    update,
    own,
    sib,
    stage,
    landed,
    mom,
    rounded,
    counts,
    packed,
    parts1,
    chunk1,
    parts2,
    chunk2,
    full,
    load_sem,
    sib_send,
    sib_recv,
    ring_send,
    ring_recv,
    send1,
    recv1,
    send2,
    recv2,
    send3,
    recv3,
):
    mats, rows, cols = mom.shape
    strip = cols // side
    replica = lax.axis_index("replica")
    fsdp = lax.axis_index("fsdp")
    y, core = replica // 2, lax.rem(replica, 2)
    x, z = fsdp // side, lax.rem(fsdp, side)
    sibling = (2 * y + 1 - core, fsdp)

    def along(axis, d, which):
        if axis == 0:
            return (2 * y + which, lax.rem(x + d, side) * side + z)
        return (2 * y + which, x * side + lax.rem(z + d, side))

    far_first = sorted(range(1, side), key=lambda d: -min(d, side - d))
    barrier = pltpu.get_barrier_semaphore()

    def greet(peer):
        pl.semaphore_signal(barrier, inc=1, device_id=peer, device_id_type=MESH)

    steps = (1, 2, ring - 2, ring - 1)
    greet(sibling)
    for d in steps:
        greet((2 * lax.rem(y + d, ring) + core, fsdp))
    lines = [(axis, d) for d in far_first for axis in (0, 1)]
    for axis, d in lines:
        greet(along(axis, d, 1))

    @pl.when(core == 1)
    def _():
        for axis, d in lines:
            greet(along(axis, d, 0))

    order = [ring // 2]
    for hops in range(ring // 2 - 1, 0, -1):
        order += [hops, ring - hops]
    order += [0]

    def chunk_of(o, which):
        return pl.ds((2 * lax.rem(y + o, ring) + which) * mats, mats)

    loads = {}
    for o in order:
        loads[o] = pltpu.make_async_copy(
            grad.at[0, chunk_of(o, core)], own.at[o], load_sem.at[o]
        )
        loads[o].start()
    load_mom = pltpu.make_async_copy(momentum, mom, load_sem.at[ring])
    load_mom.start()
    load_counts = pltpu.make_async_copy(row_counts, counts, load_sem.at[ring + 1])
    load_counts.start()

    pl.semaphore_wait(barrier, 1 + len(steps) + (1 + core) * len(lines))

    exchange = {}
    for o in order:
        exchange[o] = pltpu.make_async_remote_copy(
            src_ref=grad.at[0, chunk_of(o, 1 - core)],
            dst_ref=sib.at[o],
            send_sem=sib_send.at[o],
            recv_sem=sib_recv.at[o],
            device_id=sibling,
            device_id_type=MESH,
        )
        exchange[o].start()

    ready = set()

    def pair_sum(o, j):
        if o not in ready:
            loads[o].wait()
            exchange[o].wait_recv()
            ready.add(o)
        return own[o, j].astype(F32) + sib[o, j].astype(F32)

    hop = {}

    def arrivals(way, hops, j, value):
        for before, after in ROUTES[j].items():
            slot = slots.get((way, before, j))
            if after == hops and slot is not None:
                hop[slot].wait_recv()
                value = value + landed[slot].astype(F32)
        return value

    def ring_step(hops, j):
        for way in (0, 1):
            slot = slots.get((way, hops, j))
            if slot is None:
                continue
            value = arrivals(way, hops, j, pair_sum(hops if way == 0 else ring - hops, j))
            stage[slot] = value.astype(BF16)
            step = hops - ROUTES[j][hops]
            to = lax.rem(y + (step if way == 0 else ring - step), ring)
            hop[slot] = pltpu.make_async_remote_copy(
                src_ref=stage.at[slot],
                dst_ref=landed.at[slot],
                send_sem=ring_send.at[slot],
                recv_sem=ring_recv.at[slot],
                device_id=(2 * to + core, fsdp),
                device_id_type=MESH,
            )
            hop[slot].start()

    row = fsdp * rows + lax.broadcasted_iota(jnp.int32, (rows, cols), 0)
    down = lax.broadcasted_iota(jnp.int32, (cols, cols), 0)
    across = lax.broadcasted_iota(jnp.int32, (cols, cols), 1)
    eye = (down == across).astype(F32)

    def finish_sum(j):
        value = pair_sum(0, j)
        for way in (0, 1):
            value = arrivals(way, 0, j, value)
        moved = jnp.where(row < counts[replica * mats + j], 0.95 * mom[j] + value, 0.0)
        new_momentum[j] = moved
        r = moved.astype(BF16)
        rounded[j] = r
        return lax.dot_general(r, r, (((0,), (0,)), ((), ())), preferred_element_type=F32)

    def place(axis):
        return x if axis == 0 else z

    def remote(src, dst, send_sem, recv_sem, to):
        return pltpu.make_async_remote_copy(
            src_ref=src,
            dst_ref=dst,
            send_sem=send_sem,
            recv_sem=recv_sem,
            device_id=to,
            device_id_type=MESH,
        )

    def to_owner(a, d):
        return remote(
            packed.at[a, lax.rem(place(a) + d, side)],
            parts1.at[core, a, d],
            send1.at[a, d],
            recv1.at[core, a, d],
            along(a, d, 1),
        )

    def from_partner(which, a, d):
        return remote(
            packed.at[a, 0],
            parts1.at[which, a, d],
            send1.at[a, d],
            recv1.at[which, a, d],
            along(a, d, 1),
        )

    def across_owners(a, d):
        return remote(
            chunk1.at[a], parts2.at[a, d - 1], send2.at[a, d], recv2.at[a, d], along(1 - a, d, 1)
        )

    def to_user(which, a, d):
        return remote(
            chunk2.at[a, which],
            full.at[a, place(a)],
            send3.at[which, a, d],
            recv3.at[a, d],
            along(a, d, which),
        )

    def pack(a, first, second):
        tile = jnp.where(down >= across, first, second)
        diagonal = jnp.sum(second * eye, axis=0, keepdims=True)
        for index in range(side):
            packed[a, index, :strip] = tile[index * strip : (index + 1) * strip]
            packed[a, index, strip:] = diagonal

    def unpack(a):
        tile = jnp.concatenate([full[a, index, :strip] for index in range(side)], axis=0)
        turned = tile.T
        first = jnp.where(down >= across, tile, turned)
        second = jnp.where(down < across, tile, turned)
        return [first, jnp.where(down == across, full[a, 0, strip:], second)]

    for hops, chosen in ORDER:
        for j in chosen:
            ring_step(hops, j)
    load_mom.wait()
    load_counts.wait()
    pairs = range(mats // 2)
    for a in pairs:
        pack(a, finish_sum(2 * a), finish_sum(2 * a + 1))
        for d in far_first:
            to_owner(a, d).start()

        @pl.when(core == 0)
        def _():
            to_owner(a, 0).start()

    for copy in list(exchange.values()) + list(hop.values()):
        copy.wait_send()

    @pl.when(core == 1)
    def _():
        for a in pairs:
            value = packed[a, place(a)]
            for d in reversed(far_first):
                from_partner(1, a, d).wait_recv()
                value = value + parts1[1, a, d]
            chunk1[a, 1] = value
            from_partner(0, a, 0).wait_recv()
            value = parts1[0, a, 0]
            for d in reversed(far_first):
                from_partner(0, a, d).wait_recv()
                value = value + parts1[0, a, d]
            chunk1[a, 0] = value
            for d in far_first:
                across_owners(a, d).start()
        for a in pairs:
            value = chunk1[a]
            for d in reversed(far_first):
                across_owners(a, d).wait_recv()
                value = value + parts2[a, d - 1]
            chunk2[a] = value
            full[a, place(a)] = value[1]
            for d in far_first:
                to_user(0, a, d).start()
                to_user(1, a, d).start()
            to_user(0, a, 0).start()

    @pl.when(core == 0)
    def _():
        for a in pairs:
            to_user(0, a, 0).wait_recv()

    for a in pairs:
        for d in reversed(far_first):
            to_user(0, a, d).wait_recv()

    grams, scales = [], []
    for j, gram in enumerate(unpack(0) + unpack(1)):
        trace = jnp.sum(gram * eye, axis=(0, 1), keepdims=True)
        inverse = 1.0 / (jnp.sqrt(trace) + 1e-07)
        grams.append(gram * inverse * inverse)
        count = jnp.full((1, 1), counts[replica * mats + j], jnp.int32)
        scales.append(0.2 * jnp.sqrt(count.astype(F32)) * inverse)
    for j, value in enumerate(iterate([rounded[j] for j in range(mats)], grams, eye)):
        update[j] = (value * scales[j]).astype(BF16)

    for a in pairs:
        for d in far_first:
            to_owner(a, d).wait_send()

    @pl.when(core == 0)
    def _():
        for a in pairs:
            to_owner(a, 0).wait_send()

    @pl.when(core == 1)
    def _():
        for a in pairs:
            for d in far_first:
                across_owners(a, d).wait_send()
                to_user(0, a, d).wait_send()
                to_user(1, a, d).wait_send()
            to_user(0, a, 0).wait_send()


def solution(mesh):
    ring = mesh.shape["replica"] // 2
    side = 8

    def per_device(grad_part, momentum, row_counts):
        mats, rows, cols = momentum.shape
        slots = ring_messages(ring, mats)
        pairs = mats // 2
        piece = (cols // side + 1, cols)
        block = (mats, rows, cols)
        dma = pltpu.SemaphoreType.DMA
        return pl.pallas_call(
            functools.partial(kernel, ring, side, slots),
            out_shape=(
                pltpu.VMEM(block, F32),
                pltpu.VMEM(block, BF16),
            ),
            in_specs=[pl.BlockSpec(memory_space=pltpu.HBM)] * 3,
            out_specs=[pl.BlockSpec(memory_space=pltpu.VMEM)] * 2,
            scratch_shapes=[
                pltpu.VMEM((ring,) + block, BF16),
                pltpu.VMEM((ring,) + block, BF16),
                pltpu.VMEM((len(slots), rows, cols), BF16),
                pltpu.VMEM((len(slots), rows, cols), BF16),
                pltpu.VMEM(block, F32),
                pltpu.VMEM(block, BF16),
                pltpu.SMEM(row_counts.shape, jnp.int32),
                pltpu.VMEM((pairs, side) + piece, F32),
                pltpu.VMEM((2, pairs, side) + piece, F32),
                pltpu.VMEM((pairs, 2) + piece, F32),
                pltpu.VMEM((pairs, side - 1, 2) + piece, F32),
                pltpu.VMEM((pairs, 2) + piece, F32),
                pltpu.VMEM((pairs, side) + piece, F32),
                dma((ring + 2,)),
                dma((ring,)),
                dma((ring,)),
                dma((len(slots),)),
                dma((len(slots),)),
                dma((pairs, side)),
                dma((2, pairs, side)),
                dma((pairs, side)),
                dma((pairs, side)),
                dma((2, pairs, side)),
                dma((pairs, side)),
            ],
            compiler_params=pltpu.CompilerParams(
                collective_id=0, has_side_effects=True, vmem_limit_bytes=60 * 1024 * 1024
            ),
        )(grad_part, momentum, row_counts)

    return jax.shard_map(
        per_device,
        mesh=mesh,
        in_specs=(P("replica", None, "fsdp", None), P("replica", "fsdp", None), P()),
        out_specs=(P("replica", "fsdp", None), P("replica", "fsdp", None)),
        check_vma=False,
    )
```

```python
import functools

import jax
import jax.numpy as jnp
from jax import lax
from jax.experimental import pallas as pl
from jax.experimental.pallas import tpu as pltpu
from jax.sharding import PartitionSpec as P

ITERS = 3
MESH = pl.DeviceIdType.MESH
F32 = jnp.float32
BF16 = jnp.bfloat16
COEF = (3.4445, -4.775, 2.0315)


THREE_STEPS = {4: 2, 3: 2, 2: 1, 1: 0}
TWO_STEPS = {4: 2, 3: 2, 2: 0, 1: 0}
ROUTES = (THREE_STEPS, THREE_STEPS, TWO_STEPS, TWO_STEPS)
ORDER = (
    (4, (0, 1)),
    (3, (0, 1)),
    (4, (2, 3)),
    (3, (2, 3)),
    (2, (0, 1)),
    (1, (2, 3)),
    (2, (2, 3)),
    (1, (0, 1)),
)


def ring_messages(ring, mats):
    slots = {}
    for matrix in range(mats):
        for hops in range(ring // 2, 0, -1):
            for way in (0, 1):
                if hops < ring // 2 or matrix % 2 == way:
                    slots[way, hops, matrix] = len(slots)
    return slots


def split(a):
    high = a.astype(BF16)
    return high, (a - high.astype(F32)).astype(BF16)


def product(a, b):
    a_high, a_low = split(a)
    b_high, b_low = split(b)
    return jnp.dot(
        jnp.concatenate([a_high, a_low, a_high], axis=1),
        jnp.concatenate([b_high, b_high, b_low], axis=0),
        preferred_element_type=F32,
    )


def iterate(rows, grams, eye):
    total = None
    for step in range(ITERS):
        squares = [product(g, g) for g in grams]
        factors = [COEF[0] * eye + COEF[1] * g + COEF[2] * s for g, s in zip(grams, squares)]
        if step == ITERS - 1:
            break
        halves = [product(g, f) for g, f in zip(grams, factors)]
        grams = [product(h, f) for h, f in zip(halves, factors)]
        total = factors if total is None else [product(t, f) for t, f in zip(total, factors)]
    partly = []
    for r, t in zip(rows, total):
        high, low = split(t)
        partly.append(
            jnp.dot(
                jnp.concatenate([r, r], axis=1),
                jnp.concatenate([high, low], axis=0),
                preferred_element_type=F32,
            )
        )
    return [product(p, f) for p, f in zip(partly, factors)]


def kernel(
    ring,
    side,
    slots,
    grad,
    momentum,
    row_counts,
    new_momentum,
    update,
    own,
    sib,
    stage,
    landed,
    mom,
    rounded,
    counts,
    packed,
    parts1,
    chunk1,
    parts2,
    chunk2,
    full,
    load_sem,
    sib_send,
    sib_recv,
    ring_send,
    ring_recv,
    send1,
    recv1,
    send2,
    recv2,
    send3,
    recv3,
):
    mats, rows, cols = mom.shape
    strip = cols // side
    replica = lax.axis_index("replica")
    fsdp = lax.axis_index("fsdp")
    y, core = replica // 2, lax.rem(replica, 2)
    x, z = fsdp // side, lax.rem(fsdp, side)
    sibling = (2 * y + 1 - core, fsdp)

    def along(axis, d):
        if axis == 0:
            return (replica, lax.rem(x + d, side) * side + z)
        return (replica, x * side + lax.rem(z + d, side))

    far_first = sorted(range(1, side), key=lambda d: -min(d, side - d))
    barrier = pltpu.get_barrier_semaphore()

    def greet(peer):
        pl.semaphore_signal(barrier, inc=1, device_id=peer, device_id_type=MESH)

    steps = (1, 2, ring - 2, ring - 1)
    greet(sibling)
    for d in steps:
        greet((2 * lax.rem(y + d, ring) + core, fsdp))
    lines = [(axis, d) for d in far_first for axis in (0, 1)]
    for axis, d in lines:
        greet(along(axis, d))

    order = [ring // 2]
    for hops in range(ring // 2 - 1, 0, -1):
        order += [hops, ring - hops]
    order += [0]

    def chunk_of(o, which):
        return pl.ds((2 * lax.rem(y + o, ring) + which) * mats, mats)

    loads = {}
    for o in order:
        loads[o] = pltpu.make_async_copy(
            grad.at[0, chunk_of(o, core)], own.at[o], load_sem.at[o]
        )
        loads[o].start()
    load_mom = pltpu.make_async_copy(momentum, mom, load_sem.at[ring])
    load_mom.start()
    load_counts = pltpu.make_async_copy(row_counts, counts, load_sem.at[ring + 1])
    load_counts.start()

    pl.semaphore_wait(barrier, 1 + len(steps) + len(lines))

    exchange = {}
    for o in order:
        exchange[o] = pltpu.make_async_remote_copy(
            src_ref=grad.at[0, chunk_of(o, 1 - core)],
            dst_ref=sib.at[o],
            send_sem=sib_send.at[o],
            recv_sem=sib_recv.at[o],
            device_id=sibling,
            device_id_type=MESH,
        )
        exchange[o].start()

    ready = set()

    def pair_sum(o, j):
        if o not in ready:
            loads[o].wait()
            exchange[o].wait_recv()
            ready.add(o)
        return own[o, j].astype(F32) + sib[o, j].astype(F32)

    hop = {}

    def arrivals(way, hops, j, value):
        for before, after in ROUTES[j].items():
            slot = slots.get((way, before, j))
            if after == hops and slot is not None:
                hop[slot].wait_recv()
                value = value + landed[slot].astype(F32)
        return value

    def ring_step(hops, j):
        for way in (0, 1):
            slot = slots.get((way, hops, j))
            if slot is None:
                continue
            value = arrivals(way, hops, j, pair_sum(hops if way == 0 else ring - hops, j))
            stage[slot] = value.astype(BF16)
            step = hops - ROUTES[j][hops]
            to = lax.rem(y + (step if way == 0 else ring - step), ring)
            hop[slot] = pltpu.make_async_remote_copy(
                src_ref=stage.at[slot],
                dst_ref=landed.at[slot],
                send_sem=ring_send.at[slot],
                recv_sem=ring_recv.at[slot],
                device_id=(2 * to + core, fsdp),
                device_id_type=MESH,
            )
            hop[slot].start()

    row = fsdp * rows + lax.broadcasted_iota(jnp.int32, (rows, cols), 0)
    down = lax.broadcasted_iota(jnp.int32, (cols, cols), 0)
    across = lax.broadcasted_iota(jnp.int32, (cols, cols), 1)
    eye = (down == across).astype(F32)

    def finish_sum(j):
        value = pair_sum(0, j)
        for way in (0, 1):
            value = arrivals(way, 0, j, value)
        moved = jnp.where(row < counts[replica * mats + j], 0.95 * mom[j] + value, 0.0)
        new_momentum[j] = moved
        r = moved.astype(BF16)
        rounded[j] = r
        return lax.dot_general(r, r, (((0,), (0,)), ((), ())), preferred_element_type=F32)

    def place(axis):
        return x if axis == 0 else z

    def remote(src, dst, send_sem, recv_sem, to):
        return pltpu.make_async_remote_copy(
            src_ref=src,
            dst_ref=dst,
            send_sem=send_sem,
            recv_sem=recv_sem,
            device_id=to,
            device_id_type=MESH,
        )

    def to_owner(a, d):
        return remote(
            packed.at[a, lax.rem(place(a) + d, side)],
            parts1.at[a, d - 1],
            send1.at[a, d],
            recv1.at[a, d],
            along(a, d),
        )

    def across_owners(a, d):
        return remote(
            chunk1.at[a], parts2.at[a, d - 1], send2.at[a, d], recv2.at[a, d], along(1 - a, d)
        )

    def to_user(a, d):
        return remote(
            chunk2.at[a], full.at[a, place(a)], send3.at[a, d], recv3.at[a, d], along(a, d)
        )

    def pack(a, first, second):
        tile = jnp.where(down >= across, first, second)
        diagonal = jnp.sum(second * eye, axis=0, keepdims=True)
        for index in range(side):
            packed[a, index, :strip] = tile[index * strip : (index + 1) * strip]
            packed[a, index, strip:] = diagonal

    def unpack(a):
        tile = jnp.concatenate([full[a, index, :strip] for index in range(side)], axis=0)
        turned = tile.T
        first = jnp.where(down >= across, tile, turned)
        second = jnp.where(down < across, tile, turned)
        return [first, jnp.where(down == across, full[a, 0, strip:], second)]

    for hops, chosen in ORDER:
        for j in chosen:
            ring_step(hops, j)
    load_mom.wait()
    load_counts.wait()
    pairs = range(mats // 2)
    for a in pairs:
        pack(a, finish_sum(2 * a), finish_sum(2 * a + 1))
        for d in far_first:
            to_owner(a, d).start()
    for copy in list(exchange.values()) + list(hop.values()):
        copy.wait_send()
    for a in pairs:
        value = packed[a, place(a)]
        for d in reversed(far_first):
            to_owner(a, d).wait_recv()
            value = value + parts1[a, d - 1]
        chunk1[a] = value
        for d in far_first:
            across_owners(a, d).start()
    for a in pairs:
        for d in far_first:
            to_owner(a, d).wait_send()
    for a in pairs:
        value = chunk1[a]
        for d in reversed(far_first):
            across_owners(a, d).wait_recv()
            value = value + parts2[a, d - 1]
        chunk2[a] = value
        full[a, place(a)] = value
        for d in far_first:
            to_user(a, d).start()
    for a in pairs:
        for d in far_first:
            across_owners(a, d).wait_send()
    for a in pairs:
        for d in reversed(far_first):
            to_user(a, d).wait_recv()

    grams, scales = [], []
    for j, gram in enumerate(unpack(0) + unpack(1)):
        trace = jnp.sum(gram * eye, axis=(0, 1), keepdims=True)
        inverse = 1.0 / (jnp.sqrt(trace) + 1e-07)
        grams.append(gram * inverse * inverse)
        count = jnp.full((1, 1), counts[replica * mats + j], jnp.int32)
        scales.append(0.2 * jnp.sqrt(count.astype(F32)) * inverse)
    for j, value in enumerate(iterate([rounded[j] for j in range(mats)], grams, eye)):
        update[j] = (value * scales[j]).astype(BF16)

    for a in pairs:
        for d in far_first:
            to_user(a, d).wait_send()


def solution(mesh):
    ring = mesh.shape["replica"] // 2
    side = 8

    def per_device(grad_part, momentum, row_counts):
        mats, rows, cols = momentum.shape
        slots = ring_messages(ring, mats)
        pairs = mats // 2
        piece = (cols // side + 1, cols)
        block = (mats, rows, cols)
        dma = pltpu.SemaphoreType.DMA
        return pl.pallas_call(
            functools.partial(kernel, ring, side, slots),
            out_shape=(
                pltpu.VMEM(block, F32),
                pltpu.VMEM(block, BF16),
            ),
            in_specs=[pl.BlockSpec(memory_space=pltpu.HBM)] * 3,
            out_specs=[pl.BlockSpec(memory_space=pltpu.VMEM)] * 2,
            scratch_shapes=[
                pltpu.VMEM((ring,) + block, BF16),
                pltpu.VMEM((ring,) + block, BF16),
                pltpu.VMEM((len(slots), rows, cols), BF16),
                pltpu.VMEM((len(slots), rows, cols), BF16),
                pltpu.VMEM(block, F32),
                pltpu.VMEM(block, BF16),
                pltpu.SMEM(row_counts.shape, jnp.int32),
                pltpu.VMEM((pairs, side) + piece, F32),
                pltpu.VMEM((pairs, side - 1) + piece, F32),
                pltpu.VMEM((pairs,) + piece, F32),
                pltpu.VMEM((pairs, side - 1) + piece, F32),
                pltpu.VMEM((pairs,) + piece, F32),
                pltpu.VMEM((pairs, side) + piece, F32),
                dma((ring + 2,)),
                dma((ring,)),
                dma((ring,)),
                dma((len(slots),)),
                dma((len(slots),)),
                dma((pairs, side)),
                dma((pairs, side)),
                dma((pairs, side)),
                dma((pairs, side)),
                dma((pairs, side)),
                dma((pairs, side)),
            ],
            compiler_params=pltpu.CompilerParams(
                collective_id=0, has_side_effects=True, vmem_limit_bytes=60 * 1024 * 1024
            ),
        )(grad_part, momentum, row_counts)

    return jax.shard_map(
        per_device,
        mesh=mesh,
        in_specs=(P("replica", None, "fsdp", None), P("replica", "fsdp", None), P()),
        out_specs=(P("replica", "fsdp", None), P("replica", "fsdp", None)),
        check_vma=False,
    )
```

```python
import functools

import jax
import jax.numpy as jnp
from jax import lax
from jax.experimental import pallas as pl
from jax.experimental.pallas import tpu as pltpu
from jax.sharding import PartitionSpec as P

ITERS = 3
MESH = pl.DeviceIdType.MESH
F32 = jnp.float32
BF16 = jnp.bfloat16
COEF = (3.4445, -4.775, 2.0315)


THREE_STEPS = {4: 2, 3: 2, 2: 1, 1: 0}
TWO_STEPS = {4: 2, 3: 2, 2: 0, 1: 0}
ROUTES = (THREE_STEPS, THREE_STEPS, TWO_STEPS, TWO_STEPS)
ORDER = (
    (4, (0, 1)),
    (3, (0, 1)),
    (4, (2, 3)),
    (3, (2, 3)),
    (2, (0, 1)),
    (1, (2, 3)),
    (2, (2, 3)),
    (1, (0, 1)),
)


def ring_messages(ring, mats):
    slots = {}
    for matrix in range(mats):
        for hops in range(ring // 2, 0, -1):
            for way in (0, 1):
                if hops < ring // 2 or matrix % 2 == way:
                    slots[way, hops, matrix] = len(slots)
    return slots


def split(a):
    high = a.astype(BF16)
    return high, (a - high.astype(F32)).astype(BF16)


def product(a, b):
    a_high, a_low = split(a)
    b_high, b_low = split(b)
    return jnp.dot(
        jnp.concatenate([a_high, a_low, a_high], axis=1),
        jnp.concatenate([b_high, b_high, b_low], axis=0),
        preferred_element_type=F32,
    )


def iterate(rows, grams, eye):
    norms = [jnp.sqrt(jnp.sum(g * eye, axis=(0, 1), keepdims=True)) for g in grams]
    inverses = [1.0 / (n + 1e-07) for n in norms]
    total = None
    for step in range(ITERS):
        squares = [product(g, g) for g in grams]
        if step == 0:
            scales = [i * i for i in inverses]
            grams = [s * g for s, g in zip(scales, grams)]
            squares = [s * (s * h) for s, h in zip(scales, squares)]
        factors = [COEF[0] * eye + COEF[1] * g + COEF[2] * h for g, h in zip(grams, squares)]
        if step == ITERS - 1:
            break
        halves = [product(g, f) for g, f in zip(grams, factors)]
        grams = [product(h, f) for h, f in zip(halves, factors)]
        total = factors if total is None else [product(t, f) for t, f in zip(total, factors)]
    partly = []
    for r, t in zip(rows, total):
        high, low = split(t)
        partly.append(
            jnp.dot(
                jnp.concatenate([r, r], axis=1),
                jnp.concatenate([high, low], axis=0),
                preferred_element_type=F32,
            )
        )
    return [product(p, f) * i for p, f, i in zip(partly, factors, inverses)]


def kernel(
    ring,
    side,
    slots,
    grad,
    momentum,
    row_counts,
    new_momentum,
    update,
    own,
    sib,
    stage,
    landed,
    mom,
    rounded,
    counts,
    packed,
    parts1,
    chunk1,
    parts2,
    chunk2,
    full,
    load_sem,
    sib_send,
    sib_recv,
    ring_send,
    ring_recv,
    send1,
    recv1,
    send2,
    recv2,
    send3,
    recv3,
):
    mats, rows, cols = mom.shape
    strip = cols // side
    replica = lax.axis_index("replica")
    fsdp = lax.axis_index("fsdp")
    y, core = replica // 2, lax.rem(replica, 2)
    x, z = fsdp // side, lax.rem(fsdp, side)
    sibling = (2 * y + 1 - core, fsdp)

    def along(axis, d):
        if axis == 0:
            return (replica, lax.rem(x + d, side) * side + z)
        return (replica, x * side + lax.rem(z + d, side))

    far_first = sorted(range(1, side), key=lambda d: -min(d, side - d))
    barrier = pltpu.get_barrier_semaphore()

    def greet(peer):
        pl.semaphore_signal(barrier, inc=1, device_id=peer, device_id_type=MESH)

    steps = (1, 2, ring - 2, ring - 1)
    greet(sibling)
    for d in steps:
        greet((2 * lax.rem(y + d, ring) + core, fsdp))
    lines = [(axis, d) for d in far_first for axis in (0, 1)]
    for axis, d in lines:
        greet(along(axis, d))

    order = [ring // 2]
    for hops in range(ring // 2 - 1, 0, -1):
        order += [hops, ring - hops]
    order += [0]

    def chunk_of(o, which):
        return pl.ds((2 * lax.rem(y + o, ring) + which) * mats, mats)

    loads = {}
    for o in order:
        loads[o] = pltpu.make_async_copy(
            grad.at[0, chunk_of(o, core)], own.at[o], load_sem.at[o]
        )
        loads[o].start()
    load_mom = pltpu.make_async_copy(momentum, mom, load_sem.at[ring])
    load_mom.start()
    load_counts = pltpu.make_async_copy(row_counts, counts, load_sem.at[ring + 1])
    load_counts.start()

    pl.semaphore_wait(barrier, 1 + len(steps) + len(lines))

    exchange = {}
    for o in order:
        exchange[o] = pltpu.make_async_remote_copy(
            src_ref=grad.at[0, chunk_of(o, 1 - core)],
            dst_ref=sib.at[o],
            send_sem=sib_send.at[o],
            recv_sem=sib_recv.at[o],
            device_id=sibling,
            device_id_type=MESH,
        )
        exchange[o].start()

    ready = set()

    def pair_sum(o, j):
        if o not in ready:
            loads[o].wait()
            exchange[o].wait_recv()
            ready.add(o)
        return own[o, j].astype(F32) + sib[o, j].astype(F32)

    hop = {}

    def arrivals(way, hops, j, value):
        for before, after in ROUTES[j].items():
            slot = slots.get((way, before, j))
            if after == hops and slot is not None:
                hop[slot].wait_recv()
                value = value + landed[slot].astype(F32)
        return value

    def ring_step(hops, j):
        for way in (0, 1):
            slot = slots.get((way, hops, j))
            if slot is None:
                continue
            value = arrivals(way, hops, j, pair_sum(hops if way == 0 else ring - hops, j))
            stage[slot] = value.astype(BF16)
            step = hops - ROUTES[j][hops]
            to = lax.rem(y + (step if way == 0 else ring - step), ring)
            hop[slot] = pltpu.make_async_remote_copy(
                src_ref=stage.at[slot],
                dst_ref=landed.at[slot],
                send_sem=ring_send.at[slot],
                recv_sem=ring_recv.at[slot],
                device_id=(2 * to + core, fsdp),
                device_id_type=MESH,
            )
            hop[slot].start()

    row = fsdp * rows + lax.broadcasted_iota(jnp.int32, (rows, cols), 0)
    down = lax.broadcasted_iota(jnp.int32, (cols, cols), 0)
    across = lax.broadcasted_iota(jnp.int32, (cols, cols), 1)
    eye = (down == across).astype(F32)

    def finish_sum(j):
        value = pair_sum(0, j)
        for way in (0, 1):
            value = arrivals(way, 0, j, value)
        moved = jnp.where(row < counts[replica * mats + j], 0.95 * mom[j] + value, 0.0)
        new_momentum[j] = moved
        r = moved.astype(BF16)
        rounded[j] = r
        return lax.dot_general(r, r, (((0,), (0,)), ((), ())), preferred_element_type=F32)

    def place(axis):
        return x if axis == 0 else z

    def remote(src, dst, send_sem, recv_sem, to):
        return pltpu.make_async_remote_copy(
            src_ref=src,
            dst_ref=dst,
            send_sem=send_sem,
            recv_sem=recv_sem,
            device_id=to,
            device_id_type=MESH,
        )

    def to_owner(a, d):
        return remote(
            packed.at[a, lax.rem(place(a) + d, side)],
            parts1.at[a, d - 1],
            send1.at[a, d],
            recv1.at[a, d],
            along(a, d),
        )

    def across_owners(a, d):
        return remote(
            chunk1.at[a], parts2.at[a, d - 1], send2.at[a, d], recv2.at[a, d], along(1 - a, d)
        )

    def to_user(a, d):
        return remote(
            chunk2.at[a], full.at[a, place(a)], send3.at[a, d], recv3.at[a, d], along(a, d)
        )

    def pack(a, first, second):
        tile = jnp.where(down >= across, first, second)
        diagonal = jnp.sum(second * eye, axis=0, keepdims=True)
        for index in range(side):
            packed[a, index, :strip] = tile[index * strip : (index + 1) * strip]
            packed[a, index, strip:] = diagonal

    def unpack(a):
        tile = jnp.concatenate([full[a, index, :strip] for index in range(side)], axis=0)
        turned = tile.T
        first = jnp.where(down >= across, tile, turned)
        second = jnp.where(down < across, tile, turned)
        return [first, jnp.where(down == across, full[a, 0, strip:], second)]

    for hops, chosen in ORDER:
        for j in chosen:
            ring_step(hops, j)
    load_mom.wait()
    load_counts.wait()
    pairs = range(mats // 2)
    for a in reversed(pairs):
        pack(a, finish_sum(2 * a), finish_sum(2 * a + 1))
        for d in far_first:
            to_owner(a, d).start()
    for copy in list(exchange.values()) + list(hop.values()):
        copy.wait_send()
    for a in reversed(pairs):
        value = packed[a, place(a)]
        for d in reversed(far_first):
            to_owner(a, d).wait_recv()
            value = value + parts1[a, d - 1]
        chunk1[a] = value
        for d in far_first:
            across_owners(a, d).start()
    for a in pairs:
        for d in far_first:
            to_owner(a, d).wait_send()
    for a in reversed(pairs):
        value = chunk1[a]
        for d in reversed(far_first):
            across_owners(a, d).wait_recv()
            value = value + parts2[a, d - 1]
        chunk2[a] = value
        full[a, place(a)] = value
        for d in far_first:
            to_user(a, d).start()
    for a in pairs:
        for d in far_first:
            across_owners(a, d).wait_send()
    for a in pairs:
        for d in reversed(far_first):
            to_user(a, d).wait_recv()

    values = iterate([rounded[j] for j in range(mats)], unpack(0) + unpack(1), eye)
    for j, value in enumerate(values):
        count = jnp.full((1, 1), counts[replica * mats + j], jnp.int32)
        update[j] = (value * (0.2 * jnp.sqrt(count.astype(F32)))).astype(BF16)

    for a in pairs:
        for d in far_first:
            to_user(a, d).wait_send()


def solution(mesh):
    ring = mesh.shape["replica"] // 2
    side = 8

    def per_device(grad_part, momentum, row_counts):
        mats, rows, cols = momentum.shape
        slots = ring_messages(ring, mats)
        pairs = mats // 2
        piece = (cols // side + 1, cols)
        block = (mats, rows, cols)
        dma = pltpu.SemaphoreType.DMA
        return pl.pallas_call(
            functools.partial(kernel, ring, side, slots),
            out_shape=(
                pltpu.VMEM(block, F32),
                pltpu.VMEM(block, BF16),
            ),
            in_specs=[pl.BlockSpec(memory_space=pltpu.HBM)] * 3,
            out_specs=[pl.BlockSpec(memory_space=pltpu.VMEM)] * 2,
            scratch_shapes=[
                pltpu.VMEM((ring,) + block, BF16),
                pltpu.VMEM((ring,) + block, BF16),
                pltpu.VMEM((len(slots), rows, cols), BF16),
                pltpu.VMEM((len(slots), rows, cols), BF16),
                pltpu.VMEM(block, F32),
                pltpu.VMEM(block, BF16),
                pltpu.SMEM(row_counts.shape, jnp.int32),
                pltpu.VMEM((pairs, side) + piece, F32),
                pltpu.VMEM((pairs, side - 1) + piece, F32),
                pltpu.VMEM((pairs,) + piece, F32),
                pltpu.VMEM((pairs, side - 1) + piece, F32),
                pltpu.VMEM((pairs,) + piece, F32),
                pltpu.VMEM((pairs, side) + piece, F32),
                dma((ring + 2,)),
                dma((ring,)),
                dma((ring,)),
                dma((len(slots),)),
                dma((len(slots),)),
                dma((pairs, side)),
                dma((pairs, side)),
                dma((pairs, side)),
                dma((pairs, side)),
                dma((pairs, side)),
                dma((pairs, side)),
            ],
            compiler_params=pltpu.CompilerParams(
                collective_id=0, has_side_effects=True, vmem_limit_bytes=60 * 1024 * 1024
            ),
        )(grad_part, momentum, row_counts)

    return jax.shard_map(
        per_device,
        mesh=mesh,
        in_specs=(P("replica", None, "fsdp", None), P("replica", "fsdp", None), P()),
        out_specs=(P("replica", "fsdp", None), P("replica", "fsdp", None)),
        check_vma=False,
    )
```

```python
import functools

import jax
import jax.numpy as jnp
from jax import lax
from jax.experimental import pallas as pl
from jax.experimental.pallas import tpu as pltpu
from jax.sharding import PartitionSpec as P

ITERS = 3
MESH = pl.DeviceIdType.MESH
F32 = jnp.float32
BF16 = jnp.bfloat16
COEF = (3.4445, -4.775, 2.0315)


THREE_STEPS = {4: 2, 3: 2, 2: 1, 1: 0}
TWO_STEPS = {4: 2, 3: 2, 2: 0, 1: 0}
ROUTES = (THREE_STEPS, THREE_STEPS, TWO_STEPS, TWO_STEPS)
ORDER = (
    (4, (0, 1)),
    (3, (0, 1)),
    (4, (2, 3)),
    (3, (2, 3)),
    (2, (0, 1)),
    (1, (2, 3)),
    (2, (2, 3)),
    (1, (0, 1)),
)


def ring_messages(ring, mats):
    slots = {}
    for matrix in range(mats):
        for hops in range(ring // 2, 0, -1):
            for way in (0, 1):
                if hops < ring // 2 or matrix % 2 == way:
                    slots[way, hops, matrix] = len(slots)
    return slots


def split(a):
    high = a.astype(BF16)
    return high, (a - high.astype(F32)).astype(BF16)


def product(a, b):
    a_high, a_low = split(a)
    b_high, b_low = split(b)
    return jnp.dot(
        jnp.concatenate([a_high, a_low, a_high], axis=1),
        jnp.concatenate([b_high, b_high, b_low], axis=0),
        preferred_element_type=F32,
    )


def iterate(rows, grams, eye):
    norms = [jnp.sqrt(jnp.sum(g * eye, axis=(0, 1), keepdims=True)) for g in grams]
    inverses = [1.0 / (n + 1e-07) for n in norms]
    total = None
    for step in range(ITERS):
        squares = [product(g, g) for g in grams]
        if step == 0:
            scales = [i * i for i in inverses]
            grams = [s * g for s, g in zip(scales, grams)]
            squares = [s * (s * h) for s, h in zip(scales, squares)]
        factors = [COEF[0] * eye + COEF[1] * g + COEF[2] * h for g, h in zip(grams, squares)]
        if step == ITERS - 1:
            break
        halves = [product(g, f) for g, f in zip(grams, factors)]
        grams = [product(h, f) for h, f in zip(halves, factors)]
        total = factors if total is None else [product(t, f) for t, f in zip(total, factors)]
    partly = []
    for r, t in zip(rows, total):
        high, low = split(t)
        partly.append(
            jnp.dot(
                jnp.concatenate([r, r], axis=1),
                jnp.concatenate([high, low], axis=0),
                preferred_element_type=F32,
            )
        )
    return [product(p, f) * i for p, f, i in zip(partly, factors, inverses)]


def kernel(
    ring,
    side,
    slots,
    grad,
    momentum,
    row_counts,
    new_momentum,
    update,
    own,
    sib,
    stage,
    landed,
    mom,
    rounded,
    counts,
    packed,
    parts1,
    chunk1,
    parts2,
    chunk2,
    full,
    load_sem,
    sib_send,
    sib_recv,
    ring_send,
    ring_recv,
    send1,
    recv1,
    send2,
    recv2,
    send3,
    recv3,
):
    mats, rows, cols = mom.shape
    strip = cols // side
    replica = lax.axis_index("replica")
    fsdp = lax.axis_index("fsdp")
    y, core = replica // 2, lax.rem(replica, 2)
    x, z = fsdp // side, lax.rem(fsdp, side)
    sibling = (2 * y + 1 - core, fsdp)

    def along(axis, d):
        if axis == 0:
            return (replica, lax.rem(x + d, side) * side + z)
        return (replica, x * side + lax.rem(z + d, side))

    far_first = sorted(range(1, side), key=lambda d: -min(d, side - d))
    barrier = pltpu.get_barrier_semaphore()

    def greet(peer):
        pl.semaphore_signal(barrier, inc=1, device_id=peer, device_id_type=MESH)

    steps = (1, 2, ring - 2, ring - 1)
    greet(sibling)
    for d in steps:
        greet((2 * lax.rem(y + d, ring) + core, fsdp))
    lines = [(axis, d) for d in far_first for axis in (0, 1)]
    for axis, d in lines:
        greet(along(axis, d))

    order = [ring // 2]
    for hops in range(ring // 2 - 1, 0, -1):
        order += [hops, ring - hops]
    order += [0]

    def chunk_of(o, which):
        return pl.ds((2 * lax.rem(y + o, ring) + which) * mats, mats)

    loads = {}
    for o in order:
        loads[o] = pltpu.make_async_copy(
            grad.at[0, chunk_of(o, core)], own.at[o], load_sem.at[o]
        )
        loads[o].start()
    load_mom = pltpu.make_async_copy(momentum, mom, load_sem.at[ring])
    load_mom.start()
    load_counts = pltpu.make_async_copy(row_counts, counts, load_sem.at[ring + 1])
    load_counts.start()

    pl.semaphore_wait(barrier, 1 + len(steps) + len(lines))

    exchange = {}
    for o in order:
        exchange[o] = pltpu.make_async_remote_copy(
            src_ref=grad.at[0, chunk_of(o, 1 - core)],
            dst_ref=sib.at[o],
            send_sem=sib_send.at[o],
            recv_sem=sib_recv.at[o],
            device_id=sibling,
            device_id_type=MESH,
        )
        exchange[o].start()

    ready = set()

    def pair_sum(o, j):
        if o not in ready:
            loads[o].wait()
            exchange[o].wait_recv()
            ready.add(o)
        return own[o, j].astype(F32) + sib[o, j].astype(F32)

    hop = {}

    def arrivals(way, hops, j, value):
        for before, after in ROUTES[j].items():
            slot = slots.get((way, before, j))
            if after == hops and slot is not None:
                hop[slot].wait_recv()
                value = value + landed[slot].astype(F32)
        return value

    def ring_step(hops, j):
        for way in (0, 1):
            slot = slots.get((way, hops, j))
            if slot is None:
                continue
            value = arrivals(way, hops, j, pair_sum(hops if way == 0 else ring - hops, j))
            stage[slot] = value.astype(BF16)
            step = hops - ROUTES[j][hops]
            to = lax.rem(y + (step if way == 0 else ring - step), ring)
            hop[slot] = pltpu.make_async_remote_copy(
                src_ref=stage.at[slot],
                dst_ref=landed.at[slot],
                send_sem=ring_send.at[slot],
                recv_sem=ring_recv.at[slot],
                device_id=(2 * to + core, fsdp),
                device_id_type=MESH,
            )
            hop[slot].start()

    row = fsdp * rows + lax.broadcasted_iota(jnp.int32, (rows, cols), 0)
    down = lax.broadcasted_iota(jnp.int32, (cols, cols), 0)
    across = lax.broadcasted_iota(jnp.int32, (cols, cols), 1)
    eye = (down == across).astype(F32)

    def finish_sum(j):
        value = pair_sum(0, j)
        for way in (0, 1):
            value = arrivals(way, 0, j, value)
        moved = jnp.where(row < counts[replica * mats + j], 0.95 * mom[j] + value, 0.0)
        new_momentum[j] = moved
        r = moved.astype(BF16)
        rounded[j] = r
        return lax.dot_general(r, r, (((0,), (0,)), ((), ())), preferred_element_type=F32)

    def place(axis):
        return x if axis == 0 else z

    def remote(src, dst, send_sem, recv_sem, to):
        return pltpu.make_async_remote_copy(
            src_ref=src,
            dst_ref=dst,
            send_sem=send_sem,
            recv_sem=recv_sem,
            device_id=to,
            device_id_type=MESH,
        )

    def to_owner(a, d):
        return remote(
            packed.at[a, lax.rem(place(a) + d, side)],
            parts1.at[a, d - 1],
            send1.at[a, d],
            recv1.at[a, d],
            along(a, d),
        )

    def across_owners(a, d):
        return remote(
            chunk1.at[a], parts2.at[a, d - 1], send2.at[a, d], recv2.at[a, d], along(1 - a, d)
        )

    def to_user(a, d):
        return remote(
            chunk2.at[a], full.at[a, place(a)], send3.at[a, d], recv3.at[a, d], along(a, d)
        )

    def pack(a, first, second):
        tile = jnp.where(down >= across, first, second)
        diagonal = jnp.sum(second * eye, axis=0, keepdims=True)
        for index in range(side):
            packed[a, index, :strip] = tile[index * strip : (index + 1) * strip]
            packed[a, index, strip:] = diagonal

    def unpack(a):
        tile = jnp.concatenate([full[a, index, :strip] for index in range(side)], axis=0)
        turned = tile.T
        first = jnp.where(down >= across, tile, turned)
        second = jnp.where(down < across, tile, turned)
        return [first, jnp.where(down == across, full[a, 0, strip:], second)]

    for hops, chosen in ORDER:
        for j in chosen:
            ring_step(hops, j)
    load_mom.wait()
    load_counts.wait()
    pairs = range(mats // 2)
    for a in reversed(pairs):
        pack(a, finish_sum(2 * a), finish_sum(2 * a + 1))
        for d in far_first:
            to_owner(a, d).start()
    for a in reversed(pairs):
        value = packed[a, place(a)]
        for d in reversed(far_first):
            to_owner(a, d).wait_recv()
            value = value + parts1[a, d - 1]
        chunk1[a] = value
        for d in far_first:
            across_owners(a, d).start()
    for a in pairs:
        for d in far_first:
            to_owner(a, d).wait_send()
    for a in reversed(pairs):
        value = chunk1[a]
        for d in reversed(far_first):
            across_owners(a, d).wait_recv()
            value = value + parts2[a, d - 1]
        chunk2[a] = value
        full[a, place(a)] = value
        for d in far_first:
            to_user(a, d).start()
    for a in pairs:
        for d in far_first:
            across_owners(a, d).wait_send()
    for a in pairs:
        for d in reversed(far_first):
            to_user(a, d).wait_recv()

    for copy in list(exchange.values()) + list(hop.values()):
        copy.wait_send()
    values = iterate([rounded[j] for j in range(mats)], unpack(0) + unpack(1), eye)
    for j, value in enumerate(values):
        count = jnp.full((1, 1), counts[replica * mats + j], jnp.int32)
        update[j] = (value * (0.2 * jnp.sqrt(count.astype(F32)))).astype(BF16)

    for a in pairs:
        for d in far_first:
            to_user(a, d).wait_send()


def solution(mesh):
    ring = mesh.shape["replica"] // 2
    side = 8

    def per_device(grad_part, momentum, row_counts):
        mats, rows, cols = momentum.shape
        slots = ring_messages(ring, mats)
        pairs = mats // 2
        piece = (cols // side + 1, cols)
        block = (mats, rows, cols)
        dma = pltpu.SemaphoreType.DMA
        return pl.pallas_call(
            functools.partial(kernel, ring, side, slots),
            out_shape=(
                pltpu.VMEM(block, F32),
                pltpu.VMEM(block, BF16),
            ),
            in_specs=[pl.BlockSpec(memory_space=pltpu.HBM)] * 3,
            out_specs=[pl.BlockSpec(memory_space=pltpu.VMEM)] * 2,
            scratch_shapes=[
                pltpu.VMEM((ring,) + block, BF16),
                pltpu.VMEM((ring,) + block, BF16),
                pltpu.VMEM((len(slots), rows, cols), BF16),
                pltpu.VMEM((len(slots), rows, cols), BF16),
                pltpu.VMEM(block, F32),
                pltpu.VMEM(block, BF16),
                pltpu.SMEM(row_counts.shape, jnp.int32),
                pltpu.VMEM((pairs, side) + piece, F32),
                pltpu.VMEM((pairs, side - 1) + piece, F32),
                pltpu.VMEM((pairs,) + piece, F32),
                pltpu.VMEM((pairs, side - 1) + piece, F32),
                pltpu.VMEM((pairs,) + piece, F32),
                pltpu.VMEM((pairs, side) + piece, F32),
                dma((ring + 2,)),
                dma((ring,)),
                dma((ring,)),
                dma((len(slots),)),
                dma((len(slots),)),
                dma((pairs, side)),
                dma((pairs, side)),
                dma((pairs, side)),
                dma((pairs, side)),
                dma((pairs, side)),
                dma((pairs, side)),
            ],
            compiler_params=pltpu.CompilerParams(
                collective_id=0, has_side_effects=True, vmem_limit_bytes=60 * 1024 * 1024
            ),
        )(grad_part, momentum, row_counts)

    return jax.shard_map(
        per_device,
        mesh=mesh,
        in_specs=(P("replica", None, "fsdp", None), P("replica", "fsdp", None), P()),
        out_specs=(P("replica", "fsdp", None), P("replica", "fsdp", None)),
        check_vma=False,
    )
```
